32 devices in a mesh: sec: 4 (over y, x), tile: 4 (over z), half: 2 (over core).
Axes of the slice: x: 2, y: 2, z: 4, core: 2. Of those that a mesh axis runs over, the one named last changes fastest.
Arguments:
- sections_in: bfloat16 [8, 256, 1024], P('sec', 'tile', 'half'), parts along dimension 2, may hold values from -30 to 30
- first_kernel: bfloat16 [12, 1, 3, 3, 3], replicated, may hold values from -1.25 to 1.25
- first_bias: float32 [12], replicated, may hold values from -3 to 3
- second_kernel: bfloat16 [12, 12, 3, 3, 3], replicated, may hold values from -0.3125 to 0.3125
- second_bias: float32 [12], replicated, may hold values from -3 to 3
- head_kernel: bfloat16 [3, 12], replicated, may hold values from -1.75 to 1.75
- head_bias: float32 [3], replicated, may hold values from -3 to 3
Outputs:
- affinity: float32 [3, 8, 256, 1024], P(None, None, 'sec', ('half', 'tile')), parts along dimension 3
The draws below stay inside these ranges and needn't reach their ends.
There are 2 independent parts, one for each index of `half`. The reference program is written for one: setup_inputs(seed, part) draws one part's arguments, and reference() takes and returns one part's arrays. A program takes and returns all parts, laid end to end along the dimension named above; an argument that names none is the same for every part. Nothing has to cross between parts.
All inputs are finite; a program needn't handle non-finite values.
Results may differ from the reference program's by a relative error of at most 0.0016.
Values may be sent and summed in bfloat16 or wider, within the bound.
A program may use at most 128 MiB of HBM per device.

```python
import math
import jax
import jax.numpy as jnp
from jax import lax

SECTIONS = 8
CH = 12
AFF = 3
ROWS = 256
COLS = 512


def draw_sections_in(key, part):
    keys = jax.random.split(key, 6)
    offsets = jax.random.uniform(keys[0], (SECTIONS, 1, 1), jnp.float32, 0.5, 2.0)
    scales = jnp.exp(jax.random.uniform(keys[1], (SECTIONS, 1, 1), jnp.float32, jnp.log(0.5), jnp.log(1.5)))
    tilt = jax.random.uniform(keys[3], (SECTIONS, 1, 1), jnp.float32, 1.0, 2.0)
    band_shift = jax.random.uniform(keys[4], (SECTIONS, 8), jnp.float32, -0.5, 0.5)
    band_scale = jax.random.uniform(keys[5], (SECTIONS, 8), jnp.float32, 0.6, 1.4)
    row_pos = jnp.arange(ROWS, dtype=jnp.float32)
    band_index = jnp.arange(ROWS, dtype=jnp.int32) * 8 // ROWS
    band_onehot = (band_index[:, None] == jnp.arange(8, dtype=jnp.int32)[None, :]).astype(jnp.float32)
    row_shift = jnp.sum(band_shift[:, None, :] * band_onehot[None, :, :], axis=2)[:, :, None]
    row_scale = jnp.sum(band_scale[:, None, :] * band_onehot[None, :, :], axis=2)[:, :, None]
    trend = tilt * (2.0 * row_pos[None, :, None] / ROWS - 1.0) + row_shift
    rising = (1.0 + 2.0 * row_pos[None, :, None] / ROWS) * row_scale
    noise = jax.random.truncated_normal(keys[2], -3.5, 3.5, (SECTIONS, ROWS, COLS), jnp.float32)
    values = offsets + trend + scales * rising * noise
    return values.astype(jnp.bfloat16)


def gaussian(own_key, shape, spread, bound, kind=jnp.bfloat16):
    drawn = spread * jax.random.normal(own_key, shape, jnp.float32)
    return jnp.clip(drawn, min=-bound, max=bound).astype(kind)


def setup_inputs(seed: int = 0, part: int = 0) -> dict:
    streams_of = jax.random.split(jax.random.key(seed), 8)
    part_keys = jax.random.split(jax.random.fold_in(streams_of[7], part), 8)
    return {
        "sections_in": draw_sections_in(jax.random.fold_in(jax.random.fold_in(streams_of[7], part), 71), part),
        "first_kernel": gaussian(streams_of[1], (CH, 1, 3, 3, 3), 27 ** -0.5, 1.25),
        "first_bias": gaussian(streams_of[2], (CH,), 0.5, 3.0, jnp.float32),
        "second_kernel": gaussian(streams_of[3], (CH, CH, 3, 3, 3), (27 * CH) ** -0.5, 0.3125),
        "second_bias": gaussian(streams_of[4], (CH,), 0.5, 3.0, jnp.float32),
        "head_kernel": gaussian(streams_of[5], (AFF, CH), CH ** -0.5, 1.75),
        "head_bias": gaussian(streams_of[6], (AFF,), 0.5, 3.0, jnp.float32),
    }


def convolve(volume, kernel, padding):
    return lax.conv_general_dilated(volume, kernel, (1, 1, 1), padding, dimension_numbers=('NCDHW', 'OIDHW', 'NCDHW'), precision=lax.Precision.HIGHEST)

def reference(sections_in, first_kernel, first_bias, second_kernel, second_bias, head_kernel, head_bias):
    values = sections_in.astype(jnp.float32)
    cells_total = ROWS * COLS
    average = lax.optimization_barrier(jnp.sum(values, axis=(1, 2))) / cells_total
    variance = lax.optimization_barrier(jnp.sum(values * values, axis=(1, 2))) / cells_total - average * average
    inv_std = lax.rsqrt(variance + 1e-05)
    normed = ((values - average[:, None, None]) * inv_std[:, None, None]).astype(jnp.bfloat16)
    padded = jnp.pad(normed, ((0, 0), (0, 0), (2, 2)))
    block_cols = math.gcd(COLS, 512)
    block_count = COLS // block_cols
    first_f32 = first_kernel.astype(jnp.float32)
    second_f32 = second_kernel.astype(jnp.float32)
    head_f32 = head_kernel.astype(jnp.float32)

    def one_block(block_index):
        offset = block_index * block_cols
        window = lax.dynamic_slice_in_dim(padded, offset, block_cols + 4, 2).astype(jnp.float32)
        first_sum = convolve(window[None, None], first_f32, ((1, 1), (1, 1), (0, 0)))
        first_out = jax.nn.relu(first_sum + first_bias[None, :, None, None, None])
        col_index = offset - 1 + jnp.arange(block_cols + 2, dtype=jnp.int32)
        inside = (col_index >= 0) & (col_index < COLS)
        first_out = jnp.where(inside, first_out, jnp.zeros((), jnp.float32)).astype(jnp.bfloat16)
        first_out = lax.optimization_barrier(first_out).astype(jnp.float32)
        second_sum = convolve(first_out, second_f32, ((1, 1), (1, 1), (0, 0)))
        second_out = jax.nn.relu(second_sum + second_bias[None, :, None, None, None]).astype(jnp.bfloat16)
        second_out = lax.optimization_barrier(second_out).astype(jnp.float32)
        logits = jnp.einsum('oc,czyx->ozyx', head_f32, second_out[0], precision=lax.Precision.HIGHEST)
        return jax.nn.sigmoid(logits + head_bias[:, None, None, None])
    stacked = lax.map(one_block, jnp.arange(block_count, dtype=jnp.int32))
    return jnp.transpose(stacked, (1, 2, 3, 0, 4)).reshape(head_kernel.shape[0], SECTIONS, ROWS, COLS)
```

```python
import functools

import jax
import jax.numpy as jnp
import numpy as np
from jax import lax
from jax.experimental import pallas as pl
from jax.experimental.pallas import tpu as pltpu
from jax.sharding import PartitionSpec as P

LANES = 128
WIDE = 256
HALO_ROWS = 16
BF = jnp.bfloat16
F32 = jnp.float32


def exchange_kernel(
    secs, tiles, blocks, rows, x_ref, main, top, bottom, stats, stage, partial,
    send_m, recv_m, send_t, recv_t, send_b, recv_b, send_s, recv_s,
):
    s, t = lax.axis_index("sec"), lax.axis_index("tile")
    held = x_ref.shape[0]
    cols = x_ref.shape[2]
    staged = stage.shape[1]
    peers = secs * tiles
    home, place = t // blocks, t % blocks
    barrier = pltpu.get_barrier_semaphore()

    def greet(i, carry):
        s2, t2 = i // tiles, i % tiles

        @pl.when(jnp.logical_or(s2 != s, t2 != t))
        def _():
            pl.semaphore_signal(barrier, inc=1, device_id={"sec": s2, "tile": t2},
                                device_id_type=pl.DeviceIdType.MESH)

        return carry

    lax.fori_loop(0, peers, greet, 0)

    @pl.when(s == 0)
    def _():
        top[...] = jnp.zeros_like(top)

    @pl.when(s == secs - 1)
    def _():
        bottom[...] = jnp.zeros_like(bottom)

    sums = []
    squares = []
    for i in range(held):
        values = x_ref[i].astype(F32)
        moved = pltpu.roll(values, 2, 1)
        moved = jnp.concatenate([moved, moved[:, :LANES]], axis=1)
        if staged > rows:
            moved = jnp.concatenate(
                [moved, jnp.zeros((staged - rows, cols + LANES), F32)], axis=0)
        stage[i] = moved.astype(BF)
        col_sum = jnp.sum(values, axis=0, keepdims=True)
        col_square = jnp.sum(values * values, axis=0, keepdims=True)
        sums.append(sum(col_sum[:, c:c + LANES] for c in range(0, cols, LANES)))
        squares.append(sum(col_square[:, c:c + LANES] for c in range(0, cols, LANES)))
    packed = jnp.concatenate(
        sums + squares + [jnp.zeros((8 - 2 * held, LANES), F32)], axis=0)
    partial[...] = packed

    def remote(src, dst, send, recv, s2, t2):
        return pltpu.make_async_remote_copy(
            src_ref=src, dst_ref=dst, send_sem=send, recv_sem=recv,
            device_id={"sec": s2, "tile": t2}, device_id_type=pl.DeviceIdType.MESH)

    def begin(wanted, src, dst, send, recv, s2, t2):
        own = jnp.logical_and(s2 == s, t2 == t)

        @pl.when(jnp.logical_and(wanted, jnp.logical_not(own)))
        def _():
            remote(src, dst, send, recv, s2, t2).start()

        @pl.when(jnp.logical_and(wanted, own))
        def _():
            pltpu.make_async_copy(src, dst, recv).start()

    def sent(wanted, src, dst, send, recv, s2, t2):
        own = jnp.logical_and(s2 == s, t2 == t)

        @pl.when(jnp.logical_and(wanted, jnp.logical_not(own)))
        def _():
            remote(src, dst, send, recv, s2, t2).wait_send()

    def arrived(wanted, src, dst, send, recv, s2, t2):
        own = jnp.logical_and(s2 == s, t2 == t)

        @pl.when(jnp.logical_and(wanted, jnp.logical_not(own)))
        def _():
            remote(src, dst, send, recv, s2, t2).wait_recv()

        @pl.when(jnp.logical_and(wanted, own))
        def _():
            pltpu.make_async_copy(src, dst, recv).wait()

    pl.semaphore_wait(barrier, peers - 1)
    mine = pl.ds(s * held, held)
    goes_up = jnp.logical_and(place == 0, home > 0)
    goes_down = jnp.logical_and(place == blocks - 1, home < secs - 1)

    def out_stats(act):
        def body(i, carry):
            s2, t2 = i // tiles, i % tiles
            act(s2 >= 0, partial, stats.at[t, s], send_s.at[i], recv_s.at[s, t], s2, t2)
            return carry

        lax.fori_loop(0, peers, body, 0)

    def out_pixels(act):
        def body(t2, carry):
            window = pl.ds(pl.multiple_of(t2 * LANES, LANES), WIDE)
            act(t2 >= 0, stage.at[:, :, window], main.at[place, mine],
                send_m.at[t2], recv_m.at[s, place], home, t2)
            act(goes_up, stage.at[:, pl.ds(0, HALO_ROWS), window], bottom.at[mine],
                send_b.at[t2], recv_b.at[s], home - 1, t2)
            act(goes_down, stage.at[:, pl.ds(staged - HALO_ROWS, HALO_ROWS), window],
                top.at[mine], send_t.at[t2], recv_t.at[s], home + 1, t2)
            return carry

        lax.fori_loop(0, tiles, body, 0)

    out_pixels(begin)
    out_stats(begin)

    def in_pixels(s2, carry):
        window = pl.ds(pl.multiple_of(t * LANES, LANES), WIDE)
        theirs = pl.ds(s2 * held, held)

        def block(k, inner):
            arrived(s2 >= 0, stage.at[:, :, window], main.at[k, theirs],
                    send_m.at[0], recv_m.at[s2, k], s2, s * blocks + k)
            return inner

        lax.fori_loop(0, blocks, block, 0)
        arrived(s > 0, stage.at[:, pl.ds(staged - HALO_ROWS, HALO_ROWS), window],
                top.at[theirs], send_t.at[0], recv_t.at[s2], s2, s * blocks - 1)
        arrived(s < secs - 1, stage.at[:, pl.ds(0, HALO_ROWS), window], bottom.at[theirs],
                send_b.at[0], recv_b.at[s2], s2, (s + 1) * blocks)
        return carry

    lax.fori_loop(0, secs, in_pixels, 0)

    def in_stats(i, carry):
        s2, t2 = i // tiles, i % tiles
        arrived(s2 >= 0, partial, stats.at[t2, s2], send_s.at[0], recv_s.at[s2, t2], s2, t2)
        return carry

    lax.fori_loop(0, peers, in_stats, 0)
    out_pixels(sent)
    out_stats(sent)


def exchange(x, secs, tiles):
    held, rows, cols = x.shape
    brick_rows = rows * tiles // secs
    blocks = brick_rows // rows
    staged = max(rows, HALO_ROWS)
    sections = held * secs
    dma = pltpu.SemaphoreType.DMA
    vmem = pl.BlockSpec(memory_space=pltpu.VMEM)
    return pl.pallas_call(
        functools.partial(exchange_kernel, secs, tiles, blocks, rows),
        out_shape=[
            jax.ShapeDtypeStruct((blocks, sections, staged, WIDE), BF),
            jax.ShapeDtypeStruct((sections, HALO_ROWS, WIDE), BF),
            jax.ShapeDtypeStruct((sections, HALO_ROWS, WIDE), BF),
            jax.ShapeDtypeStruct((tiles, secs, 8, LANES), F32),
        ],
        in_specs=[vmem],
        out_specs=[vmem] * 4,
        scratch_shapes=[
            pltpu.VMEM((held, staged, cols + LANES), BF),
            pltpu.VMEM((8, LANES), F32),
            dma((tiles,)), dma((secs, blocks)),
            dma((tiles,)), dma((secs,)),
            dma((tiles,)), dma((secs,)),
            dma((secs * tiles,)), dma((secs, tiles)),
        ],
        compiler_params=pltpu.CompilerParams(
            collective_id=0, has_side_effects=True, vmem_limit_bytes=24 * 2**20),
        name="exchange",
    )(x)


SLOTS = 6
OUTSIDE = -1e30


def tables(zs, ch, aff):
    oz = ch * zs
    o_of = np.arange(oz) // zs
    z_of = np.arange(oz) % zs
    perm = np.zeros((zs * 16, zs * 16), np.float32)
    for y in range(16):
        for z in range(zs):
            perm[y * zs + z, z * 16 + y] = 1
    rows_pick = (o_of[:, None] == np.arange(ch)[None]).astype(np.float32)
    pick1 = np.tile(rows_pick, (3, 1))
    e1 = np.arange(3 * oz) // oz
    z1 = np.tile(z_of, 3)
    col = np.arange(3 * SLOTS * zs)
    b_col, slot, z_col = col // (SLOTS * zs), col // zs % SLOTS, col % zs
    place1 = (np.arange(3)[:, None] == b_col[None]).astype(np.float32)
    mask1 = np.zeros((9, 3 * oz, col.size), np.float32)
    for a in range(3):
        for e in range(3):
            mask1[a * 3 + e] = (
                (z_col[None] - z1[:, None] + 1 == a)
                & (slot[None] - e1[:, None] == e) & (slot[None] < 5))
    aux = (b_col == 1) & (slot == 5)
    bias_at = np.stack([(aux & (z_col == i)) for i in range(3)]).astype(np.float32)
    outside1 = np.where(
        aux[None] & (z_col[None] == 3 + e1[:, None]), OUTSIDE, 0.0).astype(np.float32)
    col2 = np.arange(3 * oz)
    ec = col2 // zs
    place2 = (np.arange(3 * ch)[:, None] == ec[None]).astype(np.float32)
    mask2 = np.stack(
        [(col2 % zs)[None] - z_of[:, None] + 1 == a for a in range(3)]).astype(np.float32)
    row = np.arange(aff * zs * 8)
    pick_h = ((row // (zs * 8))[:, None] == np.arange(aff)[None]).astype(np.float32)
    col_h = np.arange(8 * oz)
    place_h = (np.arange(ch)[:, None] == (col_h // zs % ch)[None]).astype(np.float32)
    mask_h = (
        ((row // 8 % zs)[:, None] == (col_h % zs)[None])
        & ((row % 8)[:, None] == (col_h // oz)[None])).astype(np.float32)
    as_bf = lambda v: jnp.asarray(v.astype(jnp.bfloat16))
    return [as_bf(v) for v in (
        perm, rows_pick, pick1, place1, mask1, bias_at[:, None, :], outside1, place2, mask2,
        pick_h, place_h, mask_h)]


def dot(a, b):
    return jnp.dot(a, b, preferred_element_type=F32)


def compute_kernel(
    secs, tiles, rows, cells, main, top, bottom, stats, k1, k2, kh, b1, b2, bh,
    perm, pick2, pick1, place1, mask1, bias_at, outside1, place2, mask2, pick_h, place_h, mask_h,
    out, w1, w2, wh, bias2, bias_h, shifted, first,
):
    s, t = lax.axis_index("sec"), lax.axis_index("tile")
    aff, zs, brick_rows, brick_cols = out.shape
    blocks, _, staged, _ = main.shape
    held = zs // secs
    ch = b1.shape[0]
    oz = ch * zs

    bias1 = jnp.concatenate(
        [jnp.full((zs, w1.shape[1]), b1[o], F32) for _ in range(3) for o in range(ch)], axis=0)
    high = bias1.astype(BF).astype(F32)
    mid = (bias1 - high).astype(BF).astype(F32)
    low = bias1 - high - mid
    built = outside1[...].astype(F32)
    for i, part in enumerate((high, mid, low)):
        built = built + part * bias_at[i].astype(F32)
    for i in range(9):
        placed = dot(dot(pick1[...], k1[i]).astype(BF), place1[...])
        built = built + placed * mask1[i].astype(F32)
    w1[...] = built.astype(BF)
    blocks_row = [[jnp.zeros((oz, 3 * oz), BF)] * 4 for _ in range(2)]
    for b in range(3):
        band = jnp.zeros((oz, 3 * oz), F32)
        for a in range(3):
            placed = dot(dot(pick2[...], k2[a * 3 + b]).astype(BF), place2[...])
            band = band + placed * mask2[a].astype(F32)
        band = band.astype(BF)
        for p in range(2):
            blocks_row[p][b + p] = band
    w2[...] = jnp.concatenate(
        [jnp.concatenate(blocks_row[p], axis=1) for p in range(2)], axis=0)
    wh[...] = (dot(dot(pick_h[...], kh[...]).astype(BF), place_h[...])
               * mask_h[...].astype(F32)).astype(BF)
    bias2[...] = jnp.concatenate(
        [jnp.full((zs, WIDE), b2[o], F32) for _ in range(2) for o in range(ch)], axis=0)
    bias_h[...] = jnp.concatenate(
        [jnp.full((zs * 8, LANES), bh[k], F32) for k in range(aff)], axis=0)

    summed = jnp.sum(stats[...], axis=0)
    summed = jnp.sum(summed, axis=2, keepdims=True)
    total = jnp.concatenate([summed[i, 0:held] for i in range(secs)], axis=0)
    square = jnp.concatenate([summed[i, held:2 * held] for i in range(secs)], axis=0)
    average = total / cells
    variance = square / cells - average * average
    inv_std = jnp.broadcast_to(lax.rsqrt(variance + 1e-05), (zs, WIDE))
    average = jnp.broadcast_to(average, (zs, WIDE))

    lane = lax.broadcasted_iota(jnp.int32, (16, zs, WIDE), 2) - 2 + t * brick_cols
    col_inside = (lane >= 0) & (lane < brick_cols * tiles)
    slot = lax.broadcasted_iota(jnp.int32, (16, zs, LANES), 1)
    x_at = lax.broadcasted_iota(jnp.int32, (16, zs, LANES), 2) + t * brick_cols
    y_in = lax.broadcasted_iota(jnp.int32, (16, zs, LANES), 0)
    x_seen = x_at + slot - 4
    x_outside = (x_seen < 0) | (x_seen >= brick_cols * tiles)

    def spread(raw, row0, inside):
        turned = dot(perm[...], raw.reshape(zs * 16, WIDE)).reshape(16, zs, WIDE)
        normed = (turned - average[None]) * inv_std[None]
        normed = jnp.where(col_inside & inside, normed, 0.0).reshape(16 * zs, WIDE)
        parts = [normed[:, :LANES]]
        for i in range(1, 5):
            parts.append(pltpu.roll(normed, WIDE - i, 1)[:, :LANES])
        y_at = y_in + row0 + s * brick_rows
        y_outside = (y_at < 0) | (y_at >= brick_rows * secs)
        aux = jnp.where(
            slot < 3, 1.0, jnp.where((slot < 6) & (y_outside | x_outside), 1.0, 0.0))
        parts = [part.reshape(16, zs, LANES) for part in parts] + [aux]
        return jnp.concatenate(parts, axis=1).astype(BF)

    step = min(rows, 16)
    for k in range(blocks):
        for q in range(staged // 16):
            row0 = k * rows + q * 16
            ready = spread(main[k, :, q * 16:q * 16 + 16, :], row0, True)
            shifted[2 + row0:2 + row0 + step] = ready[:step]
    last = rows - 2 - (staged - HALO_ROWS)
    shifted[0:2] = spread(top[...], -2 - last, s > 0)[last:last + 2]
    shifted[2 + brick_rows:4 + brick_rows] = spread(bottom[...], brick_rows, s < secs - 1)[0:2]

    depth1 = w1.shape[1]

    def layer_one(i, carry):
        j = 2 * i
        x = jnp.concatenate(
            [shifted[pl.ds(j + d, 3)].reshape(depth1, LANES) for d in range(2)], axis=1)
        y = jnp.maximum(dot(w1[...], x), 0.0).astype(BF)
        first[j] = y[:, :LANES]
        first[j + 1] = y[:, LANES:]
        return carry

    lax.fori_loop(0, (brick_rows + 2) // 2, layer_one, 0, unroll=3)

    def layer_two(i, carry):
        found = []
        for h in range(2):
            j = 8 * i + 4 * h
            x = jnp.concatenate(
                [first[pl.ds(j + d, 4)].reshape(12 * oz, LANES) for d in (0, 2)], axis=1)
            y = jnp.maximum(dot(w2[...], x) + bias2[...], 0.0).astype(BF)
            found += [y[:, :LANES], y[:, LANES:]]
        logits = dot(wh[...], jnp.concatenate(found, axis=0)) + bias_h[...]
        out[:, :, pl.ds(pl.multiple_of(8 * i, 8), 8), :] = jax.nn.sigmoid(logits).reshape(
            aff, zs, 8, LANES)
        return carry

    lax.fori_loop(0, brick_rows // 8, layer_two, 0, unroll=2)


def compute(pixels, k1, b1, k2, b2, kh, bh, secs, tiles, rows):
    main = pixels[0]
    blocks, zs = main.shape[:2]
    brick_rows = blocks * rows
    ch, aff = b1.shape[0], bh.shape[0]
    oz = ch * zs
    cells = brick_rows * secs * LANES * tiles
    k1 = jnp.transpose(k1[:, 0], (1, 3, 0, 2)).reshape(9, ch, 3)
    k2 = jnp.transpose(k2, (2, 3, 0, 4, 1)).reshape(9, ch, 3 * ch)
    consts = tables(zs, ch, aff)
    vmem = pl.BlockSpec(memory_space=pltpu.VMEM)
    smem = pl.BlockSpec(memory_space=pltpu.SMEM)
    return pl.pallas_call(
        functools.partial(compute_kernel, secs, tiles, rows, cells),
        out_shape=jax.ShapeDtypeStruct((aff, zs, brick_rows, LANES), F32),
        in_specs=[vmem] * 7 + [smem] * 3 + [vmem] * len(consts),
        out_specs=vmem,
        scratch_shapes=[
            pltpu.VMEM((3 * oz, 3 * SLOTS * zs), BF),
            pltpu.VMEM((2 * oz, 12 * oz), BF),
            pltpu.VMEM((aff * zs * 8, 8 * oz), BF),
            pltpu.VMEM((2 * oz, WIDE), F32),
            pltpu.VMEM((aff * zs * 8, LANES), F32),
            pltpu.VMEM((brick_rows + 4, SLOTS * zs, LANES), BF),
            pltpu.VMEM((brick_rows + 2, 3 * oz, LANES), BF),
        ],
        compiler_params=pltpu.CompilerParams(vmem_limit_bytes=40 * 2**20),
        name="predict",
    )(*pixels, k1, k2, kh, b1, b2, bh, *consts)


def per_device(
    sections_in, first_kernel, first_bias, second_kernel, second_bias, head_kernel, head_bias
):
    secs, tiles = lax.axis_size("sec"), lax.axis_size("tile")
    pixels = exchange(sections_in, secs, tiles)
    return compute(
        pixels, first_kernel, first_bias, second_kernel, second_bias, head_kernel, head_bias,
        secs, tiles, sections_in.shape[1])


def solution(mesh):
    in_specs = (P("sec", "tile", "half"), P(), P(), P(), P(), P(), P())
    out_specs = P(None, None, "sec", ("half", "tile"))
    return jax.shard_map(
        per_device, mesh=mesh, in_specs=in_specs, out_specs=out_specs, check_vma=False
    )
```

```python
import functools

import jax
import jax.numpy as jnp
import numpy as np
from jax import lax
from jax.experimental import pallas as pl
from jax.experimental.pallas import tpu as pltpu
from jax.sharding import PartitionSpec as P

LANES = 128
WIDE = 256
HALO_ROWS = 16
BF = jnp.bfloat16
F32 = jnp.float32


def dot(a, b):
    return jnp.dot(a, b, preferred_element_type=F32)


def build_weights(
    zs, k1, k2, kh, b1, b2, bh, pick2, pick1, place1, mask1, bias_at, outside1,
    place2, mask2, pick_h, place_h, mask_h, w1, w2, wh, bias2, bias_h,
):
    ch, aff = b1.shape[0], bh.shape[0]
    oz = ch * zs
    bias1 = jnp.concatenate(
        [jnp.full((zs, w1.shape[1]), b1[o], F32) for _ in range(3) for o in range(ch)], axis=0)
    high = bias1.astype(BF).astype(F32)
    mid = (bias1 - high).astype(BF).astype(F32)
    low = bias1 - high - mid
    built = outside1[...].astype(F32)
    for i, part in enumerate((high, mid, low)):
        built = built + part * bias_at[i].astype(F32)
    for i in range(9):
        placed = dot(dot(pick1[...], k1[i]).astype(BF), place1[...])
        built = built + placed * mask1[i].astype(F32)
    w1[...] = built.astype(BF)
    blocks_row = [[jnp.zeros((oz, 3 * oz), BF)] * 4 for _ in range(2)]
    for b in range(3):
        band = jnp.zeros((oz, 3 * oz), F32)
        for a in range(3):
            placed = dot(dot(pick2[...], k2[a * 3 + b]).astype(BF), place2[...])
            band = band + placed * mask2[a].astype(F32)
        band = band.astype(BF)
        for p in range(2):
            blocks_row[p][b + p] = band
    w2[...] = jnp.concatenate(
        [jnp.concatenate(blocks_row[p], axis=1) for p in range(2)], axis=0)
    wh[...] = (dot(dot(pick_h[...], kh[...]).astype(BF), place_h[...])
               * mask_h[...].astype(F32)).astype(BF)
    bias2[...] = jnp.concatenate(
        [jnp.full((zs, WIDE), b2[o], F32) for _ in range(2) for o in range(ch)], axis=0)
    bias_h[...] = jnp.concatenate(
        [jnp.full((zs * 8, LANES), bh[k], F32) for k in range(aff)], axis=0)


def exchange_kernel(
    secs, tiles, blocks, rows, count, *refs,
):
    far = refs[:count]
    out = refs[count]
    arrivals = refs[count + 1:count + 11]
    main, top, bottom, stats, w1, w2, wh, bias2, bias_h, perm = arrivals
    near = refs[count + 11:2 * count + 10] + (perm,)
    shifted, first, load, stage, partial = refs[2 * count + 10:2 * count + 15]
    (send_m, recv_m, send_t, recv_t, send_b, recv_b, send_s, recv_s) = refs[2 * count + 15:]
    loads = [pltpu.make_async_copy(far[i], near[i], load.at[i]) for i in range(count)]
    x_ref = near[0]
    s, t = lax.axis_index("sec"), lax.axis_index("tile")
    held = x_ref.shape[0]
    cols = x_ref.shape[2]
    staged = stage.shape[1]
    peers = secs * tiles
    home, place = t // blocks, t % blocks
    barrier = pltpu.get_barrier_semaphore()

    def greet(i, carry):
        s2, t2 = i // tiles, i % tiles

        @pl.when(jnp.logical_or(s2 != s, t2 != t))
        def _():
            pl.semaphore_signal(barrier, inc=1, device_id={"sec": s2, "tile": t2},
                                device_id_type=pl.DeviceIdType.MESH)

        return carry

    for copy in loads:
        copy.start()
    lax.fori_loop(0, peers, greet, 0)

    @pl.when(s == 0)
    def _():
        top[...] = jnp.zeros_like(top)

    @pl.when(s == secs - 1)
    def _():
        bottom[...] = jnp.zeros_like(bottom)

    loads[0].wait()
    sums = []
    squares = []
    for i in range(held):
        values = x_ref[i].astype(F32)
        moved = pltpu.roll(values, 2, 1)
        moved = jnp.concatenate([moved, moved[:, :LANES]], axis=1)
        if staged > rows:
            moved = jnp.concatenate(
                [moved, jnp.zeros((staged - rows, cols + LANES), F32)], axis=0)
        stage[i] = moved.astype(BF)
        col_sum = jnp.sum(values, axis=0, keepdims=True)
        col_square = jnp.sum(values * values, axis=0, keepdims=True)
        sums.append(sum(col_sum[:, c:c + LANES] for c in range(0, cols, LANES)))
        squares.append(sum(col_square[:, c:c + LANES] for c in range(0, cols, LANES)))
    packed = jnp.concatenate(
        sums + squares + [jnp.zeros((8 - 2 * held, LANES), F32)], axis=0)
    partial[...] = packed

    def remote(src, dst, send, recv, s2, t2):
        return pltpu.make_async_remote_copy(
            src_ref=src, dst_ref=dst, send_sem=send, recv_sem=recv,
            device_id={"sec": s2, "tile": t2}, device_id_type=pl.DeviceIdType.MESH)

    def begin(wanted, src, dst, send, recv, s2, t2):
        own = jnp.logical_and(s2 == s, t2 == t)

        @pl.when(jnp.logical_and(wanted, jnp.logical_not(own)))
        def _():
            remote(src, dst, send, recv, s2, t2).start()

        @pl.when(jnp.logical_and(wanted, own))
        def _():
            pltpu.make_async_copy(src, dst, recv).start()

    def sent(wanted, src, dst, send, recv, s2, t2):
        own = jnp.logical_and(s2 == s, t2 == t)

        @pl.when(jnp.logical_and(wanted, jnp.logical_not(own)))
        def _():
            remote(src, dst, send, recv, s2, t2).wait_send()

    def arrived(wanted, src, dst, send, recv, s2, t2):
        own = jnp.logical_and(s2 == s, t2 == t)

        @pl.when(jnp.logical_and(wanted, jnp.logical_not(own)))
        def _():
            remote(src, dst, send, recv, s2, t2).wait_recv()

        @pl.when(jnp.logical_and(wanted, own))
        def _():
            pltpu.make_async_copy(src, dst, recv).wait()

    pl.semaphore_wait(barrier, peers - 1)
    mine = pl.ds(s * held, held)
    goes_up = jnp.logical_and(place == 0, home > 0)
    goes_down = jnp.logical_and(place == blocks - 1, home < secs - 1)

    def out_stats(act):
        def body(i, carry):
            s2, t2 = i // tiles, i % tiles
            act(s2 >= 0, partial, stats.at[t, s], send_s.at[i], recv_s.at[s, t], s2, t2)
            return carry

        lax.fori_loop(0, peers, body, 0)

    def out_pixels(act):
        def body(t2, carry):
            window = pl.ds(pl.multiple_of(t2 * LANES, LANES), WIDE)
            act(t2 >= 0, stage.at[:, :, window], main.at[place, mine],
                send_m.at[t2], recv_m.at[s, place], home, t2)
            act(goes_up, stage.at[:, pl.ds(0, HALO_ROWS), window], bottom.at[mine],
                send_b.at[t2], recv_b.at[s], home - 1, t2)
            act(goes_down, stage.at[:, pl.ds(staged - HALO_ROWS, HALO_ROWS), window],
                top.at[mine], send_t.at[t2], recv_t.at[s], home + 1, t2)
            return carry

        lax.fori_loop(0, tiles, body, 0)

    out_pixels(begin)
    out_stats(begin)
    for copy in loads[1:]:
        copy.wait()
    build_weights(main.shape[1], *near[1:-1], w1, w2, wh, bias2, bias_h)

    def in_pixels(s2, carry):
        window = pl.ds(pl.multiple_of(t * LANES, LANES), WIDE)
        theirs = pl.ds(s2 * held, held)

        def block(k, inner):
            arrived(s2 >= 0, stage.at[:, :, window], main.at[k, theirs],
                    send_m.at[0], recv_m.at[s2, k], s2, s * blocks + k)
            return inner

        lax.fori_loop(0, blocks, block, 0)
        arrived(s > 0, stage.at[:, pl.ds(staged - HALO_ROWS, HALO_ROWS), window],
                top.at[theirs], send_t.at[0], recv_t.at[s2], s2, s * blocks - 1)
        arrived(s < secs - 1, stage.at[:, pl.ds(0, HALO_ROWS), window], bottom.at[theirs],
                send_b.at[0], recv_b.at[s2], s2, (s + 1) * blocks)
        return carry

    lax.fori_loop(0, secs, in_pixels, 0)

    def in_stats(i, carry):
        s2, t2 = i // tiles, i % tiles
        arrived(s2 >= 0, partial, stats.at[t2, s2], send_s.at[0], recv_s.at[s2, t2], s2, t2)
        return carry

    lax.fori_loop(0, peers, in_stats, 0)
    cells = rows * tiles * cols
    compute_kernel(secs, tiles, rows, cells, *arrivals, out, shifted, first)
    out_pixels(sent)
    out_stats(sent)


SLOTS = 6
OUTSIDE = -1e30


def tables(zs, ch, aff):
    oz = ch * zs
    o_of = np.arange(oz) // zs
    z_of = np.arange(oz) % zs
    perm = np.zeros((zs * 16, zs * 16), np.float32)
    for y in range(16):
        for z in range(zs):
            perm[y * zs + z, z * 16 + y] = 1
    rows_pick = (o_of[:, None] == np.arange(ch)[None]).astype(np.float32)
    pick1 = np.tile(rows_pick, (3, 1))
    e1 = np.arange(3 * oz) // oz
    z1 = np.tile(z_of, 3)
    col = np.arange(3 * SLOTS * zs)
    b_col, slot, z_col = col // (SLOTS * zs), col // zs % SLOTS, col % zs
    place1 = (np.arange(3)[:, None] == b_col[None]).astype(np.float32)
    mask1 = np.zeros((9, 3 * oz, col.size), np.float32)
    for a in range(3):
        for e in range(3):
            mask1[a * 3 + e] = (
                (z_col[None] - z1[:, None] + 1 == a)
                & (slot[None] - e1[:, None] == e) & (slot[None] < 5))
    aux = (b_col == 1) & (slot == 5)
    bias_at = np.stack([(aux & (z_col == i)) for i in range(3)]).astype(np.float32)
    outside1 = np.where(
        aux[None] & (z_col[None] == 3 + e1[:, None]), OUTSIDE, 0.0).astype(np.float32)
    col2 = np.arange(3 * oz)
    ec = col2 // zs
    place2 = (np.arange(3 * ch)[:, None] == ec[None]).astype(np.float32)
    mask2 = np.stack(
        [(col2 % zs)[None] - z_of[:, None] + 1 == a for a in range(3)]).astype(np.float32)
    row = np.arange(aff * zs * 8)
    pick_h = ((row // (zs * 8))[:, None] == np.arange(aff)[None]).astype(np.float32)
    col_h = np.arange(8 * oz)
    place_h = (np.arange(ch)[:, None] == (col_h // zs % ch)[None]).astype(np.float32)
    mask_h = (
        ((row // 8 % zs)[:, None] == (col_h % zs)[None])
        & ((row % 8)[:, None] == (col_h // oz)[None])).astype(np.float32)
    as_bf = lambda v: jnp.asarray(v.astype(jnp.bfloat16))
    return [as_bf(v) for v in (
        perm, rows_pick, pick1, place1, mask1, bias_at[:, None, :], outside1, place2, mask2,
        pick_h, place_h, mask_h)]


def exchange(x, k1, b1, k2, b2, kh, bh, secs, tiles):
    held, rows, cols = x.shape
    brick_rows = rows * tiles // secs
    blocks = brick_rows // rows
    staged = max(rows, HALO_ROWS)
    zs = held * secs
    ch, aff = b1.shape[0], bh.shape[0]
    oz = ch * zs
    k1 = jnp.transpose(k1[:, 0], (1, 3, 0, 2)).reshape(9, ch, 3)
    k2 = jnp.transpose(k2, (2, 3, 0, 4, 1)).reshape(9, ch, 3 * ch)
    perm, *consts = tables(zs, ch, aff)
    operands = [x, k1, k2, kh, b1, b2, bh, *consts, perm]
    dma = pltpu.SemaphoreType.DMA
    vmem = pl.BlockSpec(memory_space=pltpu.VMEM)
    hbm = pl.BlockSpec(memory_space=pltpu.HBM)
    near = [
        (pltpu.SMEM if v.ndim == 1 else pltpu.VMEM)(v.shape, v.dtype) for v in operands[:-1]]
    return pl.pallas_call(
        functools.partial(exchange_kernel, secs, tiles, blocks, rows, len(operands)),
        out_shape=jax.ShapeDtypeStruct((aff, zs, brick_rows, LANES), F32),
        in_specs=[hbm] * len(operands),
        out_specs=vmem,
        scratch_shapes=[
            pltpu.VMEM((blocks, zs, staged, WIDE), BF),
            pltpu.VMEM((zs, HALO_ROWS, WIDE), BF),
            pltpu.VMEM((zs, HALO_ROWS, WIDE), BF),
            pltpu.VMEM((tiles, secs, 8, LANES), F32),
            pltpu.VMEM((3 * oz, 3 * SLOTS * zs), BF),
            pltpu.VMEM((2 * oz, 12 * oz), BF),
            pltpu.VMEM((aff * zs * 8, 8 * oz), BF),
            pltpu.VMEM((2 * oz, WIDE), F32),
            pltpu.VMEM((aff * zs * 8, LANES), F32),
            pltpu.VMEM(perm.shape, BF),
        ] + near + [
            pltpu.VMEM((brick_rows + 4, SLOTS * zs, LANES), BF),
            pltpu.VMEM((brick_rows + 2, 3 * oz, LANES), BF),
            dma((len(operands),)),
            pltpu.VMEM((held, staged, cols + LANES), BF),
            pltpu.VMEM((8, LANES), F32),
            dma((tiles,)), dma((secs, blocks)),
            dma((tiles,)), dma((secs,)),
            dma((tiles,)), dma((secs,)),
            dma((secs * tiles,)), dma((secs, tiles)),
        ],
        compiler_params=pltpu.CompilerParams(
            collective_id=0, has_side_effects=True, vmem_limit_bytes=60 * 2**20),
        name="predict",
    )(*operands)


def compute_kernel(
    secs, tiles, rows, cells, main, top, bottom, stats, w1, w2, wh, bias2, bias_h, perm,
    out, shifted, first,
):
    s, t = lax.axis_index("sec"), lax.axis_index("tile")
    aff, zs, brick_rows, brick_cols = out.shape
    blocks, _, staged, _ = main.shape
    held = zs // secs
    oz = w1.shape[0] // 3

    summed = jnp.sum(stats[...], axis=0)
    summed = jnp.sum(summed, axis=2, keepdims=True)
    total = jnp.concatenate([summed[i, 0:held] for i in range(secs)], axis=0)
    square = jnp.concatenate([summed[i, held:2 * held] for i in range(secs)], axis=0)
    average = total / cells
    variance = square / cells - average * average
    inv_std = jnp.broadcast_to(lax.rsqrt(variance + 1e-05), (zs, WIDE))
    average = jnp.broadcast_to(average, (zs, WIDE))

    lane = lax.broadcasted_iota(jnp.int32, (16, zs, WIDE), 2) - 2 + t * brick_cols
    col_inside = (lane >= 0) & (lane < brick_cols * tiles)
    slot = lax.broadcasted_iota(jnp.int32, (16, zs, LANES), 1)
    x_at = lax.broadcasted_iota(jnp.int32, (16, zs, LANES), 2) + t * brick_cols
    y_in = lax.broadcasted_iota(jnp.int32, (16, zs, LANES), 0)
    x_seen = x_at + slot - 4
    x_outside = (x_seen < 0) | (x_seen >= brick_cols * tiles)

    def spread(raw, row0, inside):
        turned = dot(perm[...], raw.reshape(zs * 16, WIDE)).reshape(16, zs, WIDE)
        normed = (turned - average[None]) * inv_std[None]
        normed = jnp.where(col_inside & inside, normed, 0.0).reshape(16 * zs, WIDE)
        parts = [normed[:, :LANES]]
        for i in range(1, 5):
            parts.append(pltpu.roll(normed, WIDE - i, 1)[:, :LANES])
        y_at = y_in + row0 + s * brick_rows
        y_outside = (y_at < 0) | (y_at >= brick_rows * secs)
        aux = jnp.where(
            slot < 3, 1.0, jnp.where((slot < 6) & (y_outside | x_outside), 1.0, 0.0))
        parts = [part.reshape(16, zs, LANES) for part in parts] + [aux]
        return jnp.concatenate(parts, axis=1).astype(BF)

    step = min(rows, 16)
    for k in range(blocks):
        for q in range(staged // 16):
            row0 = k * rows + q * 16
            ready = spread(main[k, :, q * 16:q * 16 + 16, :], row0, True)
            shifted[2 + row0:2 + row0 + step] = ready[:step]
    last = rows - 2 - (staged - HALO_ROWS)
    shifted[0:2] = spread(top[...], -2 - last, s > 0)[last:last + 2]
    shifted[2 + brick_rows:4 + brick_rows] = spread(bottom[...], brick_rows, s < secs - 1)[0:2]

    depth1 = w1.shape[1]

    def layer_one(i, carry):
        j = 2 * i
        x = jnp.concatenate(
            [shifted[pl.ds(j + d, 3)].reshape(depth1, LANES) for d in range(2)], axis=1)
        y = jnp.maximum(dot(w1[...], x), 0.0).astype(BF)
        first[j] = y[:, :LANES]
        first[j + 1] = y[:, LANES:]
        return carry

    lax.fori_loop(0, (brick_rows + 2) // 2, layer_one, 0, unroll=3)

    def layer_two(i, carry):
        found = []
        for h in range(2):
            j = 8 * i + 4 * h
            x = jnp.concatenate(
                [first[pl.ds(j + d, 4)].reshape(12 * oz, LANES) for d in (0, 2)], axis=1)
            y = jnp.maximum(dot(w2[...], x) + bias2[...], 0.0).astype(BF)
            found += [y[:, :LANES], y[:, LANES:]]
        logits = dot(wh[...], jnp.concatenate(found, axis=0)) + bias_h[...]
        out[:, :, pl.ds(pl.multiple_of(8 * i, 8), 8), :] = jax.nn.sigmoid(logits).reshape(
            aff, zs, 8, LANES)
        return carry

    lax.fori_loop(0, brick_rows // 8, layer_two, 0, unroll=2)


def per_device(
    sections_in, first_kernel, first_bias, second_kernel, second_bias, head_kernel, head_bias
):
    secs, tiles = lax.axis_size("sec"), lax.axis_size("tile")
    return exchange(
        sections_in, first_kernel, first_bias, second_kernel, second_bias, head_kernel,
        head_bias, secs, tiles)


def solution(mesh):
    in_specs = (P("sec", "tile", "half"), P(), P(), P(), P(), P(), P())
    out_specs = P(None, None, "sec", ("half", "tile"))
    return jax.shard_map(
        per_device, mesh=mesh, in_specs=in_specs, out_specs=out_specs, check_vma=False
    )
```

```python
import functools

import jax
import jax.numpy as jnp
import numpy as np
from jax import lax
from jax.experimental import pallas as pl
from jax.experimental.pallas import tpu as pltpu
from jax.sharding import PartitionSpec as P

LANES = 128
WIDE = 256
HALO_ROWS = 16
BF = jnp.bfloat16
F32 = jnp.float32


def dot(a, b):
    return jnp.dot(a, b, preferred_element_type=F32)


def build_weights(
    zs, k1, k2, kh, b1, b2, bh, pick2, pick1, place1, mask1, bias_at, outside1,
    place2, mask2, pick_h, place_h, mask_h, w1, w2, wh, bias2, bias_h,
):
    ch, aff = b1.shape[0], bh.shape[0]
    oz = ch * zs
    bias1 = jnp.concatenate(
        [jnp.full((zs, w1.shape[1]), b1[o], F32) for _ in range(3) for o in range(ch)], axis=0)
    high = bias1.astype(BF).astype(F32)
    mid = (bias1 - high).astype(BF).astype(F32)
    low = bias1 - high - mid
    built = outside1[...].astype(F32)
    for i, part in enumerate((high, mid, low)):
        built = built + part * bias_at[i].astype(F32)
    for i in range(9):
        picked = lax.dot_general(
            pick1[...], k1[i // 3][:, i % 3, :], (((1,), (1,)), ((), ())),
            preferred_element_type=F32)
        placed = dot(picked.astype(BF), place1[...])
        built = built + placed * mask1[i].astype(F32)
    w1[...] = built.astype(BF)
    blocks_row = [[jnp.zeros((oz, 3 * oz), BF)] * 4 for _ in range(2)]
    for b in range(3):
        band = jnp.zeros((oz, 3 * oz), F32)
        for a in range(3):
            taps = jnp.concatenate([k2[:, a, b, e, :] for e in range(3)], axis=1)
            placed = dot(dot(pick2[...], taps).astype(BF), place2[...])
            band = band + placed * mask2[a].astype(F32)
        band = band.astype(BF)
        for p in range(2):
            blocks_row[p][b + p] = band
    w2[...] = jnp.concatenate(
        [jnp.concatenate(blocks_row[p], axis=1) for p in range(2)], axis=0)
    wh[...] = (dot(dot(pick_h[...], kh[...]).astype(BF), place_h[...])
               * mask_h[...].astype(F32)).astype(BF)
    bias2[...] = jnp.concatenate(
        [jnp.full((zs, WIDE), b2[o], F32) for _ in range(2) for o in range(ch)], axis=0)
    bias_h[...] = jnp.concatenate(
        [jnp.full((zs * 8, LANES), bh[k], F32) for k in range(aff)], axis=0)


def exchange_kernel(
    secs, tiles, blocks, rows, count, *refs,
):
    far = refs[:count]
    out = refs[count]
    arrivals = refs[count + 1:count + 12]
    main, edge, top, bottom, stats, w1, w2, wh, bias2, bias_h, perm = arrivals
    near = refs[count + 12:2 * count + 11] + (perm,)
    shifted, first, load, stage, partial, strip = refs[2 * count + 11:2 * count + 17]
    (send_m, recv_m, send_e, recv_e, send_t, recv_t, send_b, recv_b, send_s, recv_s) = refs[2 * count + 17:]
    loads = [pltpu.make_async_copy(far[i], near[i], load.at[i]) for i in range(count)]
    x_ref = near[0]
    s, t = lax.axis_index("sec"), lax.axis_index("tile")
    held = x_ref.shape[0]
    cols = x_ref.shape[2]
    staged = stage.shape[1]
    peers = secs * tiles
    home, place = t // blocks, t % blocks
    barrier = pltpu.get_barrier_semaphore()

    def greet(i, carry):
        s2, t2 = i // tiles, i % tiles

        @pl.when(jnp.logical_or(s2 != s, t2 != t))
        def _():
            pl.semaphore_signal(barrier, inc=1, device_id={"sec": s2, "tile": t2},
                                device_id_type=pl.DeviceIdType.MESH)

        return carry

    for copy in loads:
        copy.start()
    lax.fori_loop(0, peers, greet, 0)

    @pl.when(s == 0)
    def _():
        top[...] = jnp.zeros_like(top)

    @pl.when(s == secs - 1)
    def _():
        bottom[...] = jnp.zeros_like(bottom)

    loads[0].wait()
    sums = []
    squares = []
    groups = staged // 16
    strips = [jnp.zeros((16, LANES), F32)] * tiles
    halo_lane = lax.broadcasted_iota(jnp.int32, (16, LANES), 1) < 4
    for i in range(held):
        values = x_ref[i].astype(F32)
        moved = pltpu.roll(values, 2, 1)
        moved = jnp.concatenate([moved, moved[:, :LANES]], axis=1)
        if staged > rows:
            moved = jnp.concatenate(
                [moved, jnp.zeros((staged - rows, cols + LANES), F32)], axis=0)
        stage[i] = moved.astype(BF)
        for c in range(tiles):
            for q in range(groups):
                kept = jnp.where(
                    halo_lane, moved[16 * q:16 * q + 16, (c + 1) * LANES:(c + 2) * LANES], 0.0)
                turn = 4 * (i * groups + q)
                strips[c] = strips[c] + (pltpu.roll(kept, turn, 1) if turn else kept)
        col_sum = jnp.sum(values, axis=0, keepdims=True)
        col_square = jnp.sum(values * values, axis=0, keepdims=True)
        sums.append(sum(col_sum[:, c:c + LANES] for c in range(0, cols, LANES)))
        squares.append(sum(col_square[:, c:c + LANES] for c in range(0, cols, LANES)))
    for c in range(tiles):
        strip[c] = strips[c].astype(BF)
    packed = jnp.concatenate(
        sums + squares + [jnp.zeros((8 - 2 * held, LANES), F32)], axis=0)
    partial[...] = packed

    def remote(src, dst, send, recv, s2, t2):
        return pltpu.make_async_remote_copy(
            src_ref=src, dst_ref=dst, send_sem=send, recv_sem=recv,
            device_id={"sec": s2, "tile": t2}, device_id_type=pl.DeviceIdType.MESH)

    def begin(wanted, src, dst, send, recv, s2, t2):
        own = jnp.logical_and(s2 == s, t2 == t)

        @pl.when(jnp.logical_and(wanted, jnp.logical_not(own)))
        def _():
            remote(src, dst, send, recv, s2, t2).start()

        @pl.when(jnp.logical_and(wanted, own))
        def _():
            pltpu.make_async_copy(src, dst, recv).start()

    def sent(wanted, src, dst, send, recv, s2, t2):
        own = jnp.logical_and(s2 == s, t2 == t)

        @pl.when(jnp.logical_and(wanted, jnp.logical_not(own)))
        def _():
            remote(src, dst, send, recv, s2, t2).wait_send()

    def arrived(wanted, src, dst, send, recv, s2, t2):
        own = jnp.logical_and(s2 == s, t2 == t)

        @pl.when(jnp.logical_and(wanted, jnp.logical_not(own)))
        def _():
            remote(src, dst, send, recv, s2, t2).wait_recv()

        @pl.when(jnp.logical_and(wanted, own))
        def _():
            pltpu.make_async_copy(src, dst, recv).wait()

    pl.semaphore_wait(barrier, peers - 1)
    mine = pl.ds(s * held, held)
    goes_up = jnp.logical_and(place == 0, home > 0)
    goes_down = jnp.logical_and(place == blocks - 1, home < secs - 1)

    def out_stats(act):
        def body(i, carry):
            s2, t2 = i // tiles, i % tiles
            act(s2 >= 0, partial, stats.at[t, s], send_s.at[i], recv_s.at[s, t], s2, t2)
            return carry

        lax.fori_loop(0, peers, body, 0)

    def out_pixels(act):
        def body(t2, carry):
            window = pl.ds(pl.multiple_of(t2 * LANES, LANES), WIDE)
            block = pl.ds(pl.multiple_of(t2 * LANES, LANES), LANES)
            act(t2 >= 0, stage.at[:, :, block], main.at[place, mine],
                send_m.at[t2], recv_m.at[s, place], home, t2)
            act(t2 >= 0, strip.at[t2], edge.at[place, s],
                send_e.at[t2], recv_e.at[s, place], home, t2)
            act(goes_up, stage.at[:, pl.ds(0, HALO_ROWS), window], bottom.at[mine],
                send_b.at[t2], recv_b.at[s], home - 1, t2)
            act(goes_down, stage.at[:, pl.ds(staged - HALO_ROWS, HALO_ROWS), window],
                top.at[mine], send_t.at[t2], recv_t.at[s], home + 1, t2)
            return carry

        lax.fori_loop(0, tiles, body, 0)

    out_pixels(begin)
    out_stats(begin)
    for copy in loads[1:]:
        copy.wait()
    build_weights(main.shape[1], *near[1:-1], w1, w2, wh, bias2, bias_h)

    def in_pixels(s2, carry):
        window = pl.ds(pl.multiple_of(t * LANES, LANES), WIDE)
        columns = pl.ds(pl.multiple_of(t * LANES, LANES), LANES)
        theirs = pl.ds(s2 * held, held)

        def block(k, inner):
            arrived(s2 >= 0, stage.at[:, :, columns], main.at[k, theirs],
                    send_m.at[0], recv_m.at[s2, k], s2, s * blocks + k)
            arrived(s2 >= 0, strip.at[t], edge.at[k, s2],
                    send_e.at[0], recv_e.at[s2, k], s2, s * blocks + k)
            return inner

        lax.fori_loop(0, blocks, block, 0)
        arrived(s > 0, stage.at[:, pl.ds(staged - HALO_ROWS, HALO_ROWS), window],
                top.at[theirs], send_t.at[0], recv_t.at[s2], s2, s * blocks - 1)
        arrived(s < secs - 1, stage.at[:, pl.ds(0, HALO_ROWS), window], bottom.at[theirs],
                send_b.at[0], recv_b.at[s2], s2, (s + 1) * blocks)
        return carry

    lax.fori_loop(0, secs, in_pixels, 0)

    def in_stats(i, carry):
        s2, t2 = i // tiles, i % tiles
        arrived(s2 >= 0, partial, stats.at[t2, s2], send_s.at[0], recv_s.at[s2, t2], s2, t2)
        return carry

    lax.fori_loop(0, peers, in_stats, 0)
    cells = rows * tiles * cols
    compute_kernel(secs, tiles, rows, cells, *arrivals, out, shifted, first)
    out_pixels(sent)
    out_stats(sent)


SLOTS = 6
OUTSIDE = -1e30


def tables(zs, ch, aff):
    oz = ch * zs
    o_of = np.arange(oz) // zs
    z_of = np.arange(oz) % zs
    perm = np.zeros((zs * 16, zs * 16), np.float32)
    for y in range(16):
        for z in range(zs):
            perm[y * zs + z, z * 16 + y] = 1
    rows_pick = (o_of[:, None] == np.arange(ch)[None]).astype(np.float32)
    pick1 = np.tile(rows_pick, (3, 1))
    e1 = np.arange(3 * oz) // oz
    z1 = np.tile(z_of, 3)
    col = np.arange(3 * SLOTS * zs)
    b_col, slot, z_col = col // (SLOTS * zs), col // zs % SLOTS, col % zs
    place1 = (np.arange(3)[:, None] == b_col[None]).astype(np.float32)
    mask1 = np.zeros((9, 3 * oz, col.size), np.float32)
    for a in range(3):
        for e in range(3):
            mask1[a * 3 + e] = (
                (z_col[None] - z1[:, None] + 1 == a)
                & (slot[None] - e1[:, None] == e) & (slot[None] < 5))
    aux = (b_col == 1) & (slot == 5)
    bias_at = np.stack([(aux & (z_col == i)) for i in range(3)]).astype(np.float32)
    outside1 = np.where(
        aux[None] & (z_col[None] == 3 + e1[:, None]), OUTSIDE, 0.0).astype(np.float32)
    col2 = np.arange(3 * oz)
    ec = col2 // zs
    place2 = (np.arange(3 * ch)[:, None] == ec[None]).astype(np.float32)
    mask2 = np.stack(
        [(col2 % zs)[None] - z_of[:, None] + 1 == a for a in range(3)]).astype(np.float32)
    row = np.arange(aff * zs * 8)
    pick_h = ((row // (zs * 8))[:, None] == np.arange(aff)[None]).astype(np.float32)
    col_h = np.arange(8 * oz)
    place_h = (np.arange(ch)[:, None] == (col_h // zs % ch)[None]).astype(np.float32)
    mask_h = (
        ((row // 8 % zs)[:, None] == (col_h % zs)[None])
        & ((row % 8)[:, None] == (col_h // oz)[None])).astype(np.float32)
    as_bf = lambda v: jnp.asarray(v.astype(jnp.bfloat16))
    return [as_bf(v) for v in (
        perm, rows_pick, pick1, place1, mask1, bias_at[:, None, :], outside1, place2, mask2,
        pick_h, place_h, mask_h)]


def exchange(x, k1, b1, k2, b2, kh, bh, secs, tiles):
    held, rows, cols = x.shape
    brick_rows = rows * tiles // secs
    blocks = brick_rows // rows
    staged = max(rows, HALO_ROWS)
    zs = held * secs
    ch, aff = b1.shape[0], bh.shape[0]
    oz = ch * zs
    k1 = jnp.transpose(k1[:, 0], (1, 2, 3, 0))
    k2 = jnp.transpose(k2, (0, 2, 3, 4, 1))
    perm, *consts = tables(zs, ch, aff)
    operands = [x, k1, k2, kh, b1, b2, bh, *consts, perm]
    dma = pltpu.SemaphoreType.DMA
    vmem = pl.BlockSpec(memory_space=pltpu.VMEM)
    hbm = pl.BlockSpec(memory_space=pltpu.HBM)
    near = [
        (pltpu.SMEM if v.ndim == 1 else pltpu.VMEM)(v.shape, v.dtype) for v in operands[:-1]]
    return pl.pallas_call(
        functools.partial(exchange_kernel, secs, tiles, blocks, rows, len(operands)),
        out_shape=jax.ShapeDtypeStruct((aff, zs, brick_rows, LANES), F32),
        in_specs=[hbm] * len(operands),
        out_specs=vmem,
        scratch_shapes=[
            pltpu.VMEM((blocks, zs, staged, LANES), BF),
            pltpu.VMEM((blocks, secs, 16, LANES), BF),
            pltpu.VMEM((zs, HALO_ROWS, WIDE), BF),
            pltpu.VMEM((zs, HALO_ROWS, WIDE), BF),
            pltpu.VMEM((tiles, secs, 8, LANES), F32),
            pltpu.VMEM((3 * oz, 3 * SLOTS * zs), BF),
            pltpu.VMEM((2 * oz, 12 * oz), BF),
            pltpu.VMEM((aff * zs * 8, 8 * oz), BF),
            pltpu.VMEM((2 * oz, WIDE), F32),
            pltpu.VMEM((aff * zs * 8, LANES), F32),
            pltpu.VMEM(perm.shape, BF),
        ] + near + [
            pltpu.VMEM((brick_rows + 4, SLOTS * zs, LANES), BF),
            pltpu.VMEM((brick_rows + 2, 3 * oz, LANES), BF),
            dma((len(operands),)),
            pltpu.VMEM((held, staged, cols + LANES), BF),
            pltpu.VMEM((8, LANES), F32),
            pltpu.VMEM((tiles, 16, LANES), BF),
            dma((tiles,)), dma((secs, blocks)),
            dma((tiles,)), dma((secs, blocks)),
            dma((tiles,)), dma((secs,)),
            dma((tiles,)), dma((secs,)),
            dma((secs * tiles,)), dma((secs, tiles)),
        ],
        compiler_params=pltpu.CompilerParams(
            collective_id=0, has_side_effects=True, vmem_limit_bytes=60 * 2**20),
        name="predict",
    )(*operands)


def compute_kernel(
    secs, tiles, rows, cells, main, edge, top, bottom, stats, w1, w2, wh, bias2, bias_h, perm,
    out, shifted, first,
):
    s, t = lax.axis_index("sec"), lax.axis_index("tile")
    aff, zs, brick_rows, brick_cols = out.shape
    blocks, _, staged, _ = main.shape
    held = zs // secs
    oz = w1.shape[0] // 3

    summed = jnp.sum(stats[...], axis=0)
    summed = jnp.sum(summed, axis=2, keepdims=True)
    total = jnp.concatenate([summed[i, 0:held] for i in range(secs)], axis=0)
    square = jnp.concatenate([summed[i, held:2 * held] for i in range(secs)], axis=0)
    average = total / cells
    variance = square / cells - average * average
    inv_std = jnp.broadcast_to(lax.rsqrt(variance + 1e-05), (zs, WIDE))
    average = jnp.broadcast_to(average, (zs, WIDE))

    lane = lax.broadcasted_iota(jnp.int32, (16, zs, WIDE), 2) - 2 + t * brick_cols
    col_inside = (lane >= 0) & (lane < brick_cols * tiles)
    slot = lax.broadcasted_iota(jnp.int32, (16, zs, LANES), 1)
    x_at = lax.broadcasted_iota(jnp.int32, (16, zs, LANES), 2) + t * brick_cols
    y_in = lax.broadcasted_iota(jnp.int32, (16, zs, LANES), 0)
    x_seen = x_at + slot - 4
    x_outside = (x_seen < 0) | (x_seen >= brick_cols * tiles)

    def spread(raw, row0, inside):
        turned = dot(perm[...], raw.reshape(zs * 16, WIDE)).reshape(16, zs, WIDE)
        normed = (turned - average[None]) * inv_std[None]
        normed = jnp.where(col_inside & inside, normed, 0.0).reshape(16 * zs, WIDE)
        parts = [normed[:, :LANES]]
        for i in range(1, 5):
            parts.append(pltpu.roll(normed, WIDE - i, 1)[:, :LANES])
        y_at = y_in + row0 + s * brick_rows
        y_outside = (y_at < 0) | (y_at >= brick_rows * secs)
        aux = jnp.where(
            slot < 3, 1.0, jnp.where((slot < 6) & (y_outside | x_outside), 1.0, 0.0))
        parts = [part.reshape(16, zs, LANES) for part in parts] + [aux]
        return jnp.concatenate(parts, axis=1).astype(BF)

    step = min(rows, 16)
    for k in range(blocks):
        for q in range(staged // 16):
            row0 = k * rows + q * 16
            halo = []
            for z in range(zs):
                turn = 4 * (z % held * (staged // 16) + q)
                strip = edge[k, z // held].astype(F32)
                halo.append(pltpu.roll(strip, LANES - turn, 1) if turn else strip)
            halo = jnp.concatenate(halo, axis=0).astype(BF).reshape(zs, 16, LANES)
            ready = spread(jnp.concatenate(
                [main[k, :, q * 16:q * 16 + 16, :], halo], axis=2), row0, True)
            shifted[2 + row0:2 + row0 + step] = ready[:step]
    last = rows - 2 - (staged - HALO_ROWS)
    shifted[0:2] = spread(top[...], -2 - last, s > 0)[last:last + 2]
    shifted[2 + brick_rows:4 + brick_rows] = spread(bottom[...], brick_rows, s < secs - 1)[0:2]

    depth1 = w1.shape[1]

    def layer_one(i, carry):
        j = 2 * i
        x = jnp.concatenate(
            [shifted[pl.ds(j + d, 3)].reshape(depth1, LANES) for d in range(2)], axis=1)
        y = jnp.maximum(dot(w1[...], x), 0.0).astype(BF)
        first[j] = y[:, :LANES]
        first[j + 1] = y[:, LANES:]
        return carry

    lax.fori_loop(0, (brick_rows + 2) // 2, layer_one, 0, unroll=3)

    def layer_two(i, carry):
        found = []
        for h in range(2):
            j = 8 * i + 4 * h
            x = jnp.concatenate(
                [first[pl.ds(j + d, 4)].reshape(12 * oz, LANES) for d in (0, 2)], axis=1)
            y = jnp.maximum(dot(w2[...], x) + bias2[...], 0.0).astype(BF)
            found += [y[:, :LANES], y[:, LANES:]]
        logits = dot(wh[...], jnp.concatenate(found, axis=0)) + bias_h[...]
        out[:, :, pl.ds(pl.multiple_of(8 * i, 8), 8), :] = jax.nn.sigmoid(logits).reshape(
            aff, zs, 8, LANES)
        return carry

    lax.fori_loop(0, brick_rows // 8, layer_two, 0, unroll=2)


def per_device(
    sections_in, first_kernel, first_bias, second_kernel, second_bias, head_kernel, head_bias
):
    secs, tiles = lax.axis_size("sec"), lax.axis_size("tile")
    return exchange(
        sections_in, first_kernel, first_bias, second_kernel, second_bias, head_kernel,
        head_bias, secs, tiles)


def solution(mesh):
    in_specs = (P("sec", "tile", "half"), P(), P(), P(), P(), P(), P())
    out_specs = P(None, None, "sec", ("half", "tile"))
    return jax.shard_map(
        per_device, mesh=mesh, in_specs=in_specs, out_specs=out_specs, check_vma=False
    )
```

```python
import functools

import jax
import jax.numpy as jnp
import numpy as np
from jax import lax
from jax.experimental import pallas as pl
from jax.experimental.pallas import tpu as pltpu
from jax.sharding import PartitionSpec as P

LANES = 128
WIDE = 256
HALO_ROWS = 16
BF = jnp.bfloat16
F32 = jnp.float32


def dot(a, b):
    return jnp.dot(a, b, preferred_element_type=F32)


def build_weights(
    zs, k1, k2, kh, b1, b2, bh, pick2, pick1, place1, mask1, bias_at, outside1,
    place2, mask2, pick_h, place_h, mask_h, w1, w2, wh, bias2, bias_h,
):
    ch, aff = b1.shape[0], bh.shape[0]
    oz = ch * zs
    bias1 = jnp.concatenate(
        [jnp.full((zs, w1.shape[1]), b1[o], F32) for _ in range(3) for o in range(ch)], axis=0)
    high = bias1.astype(BF).astype(F32)
    mid = (bias1 - high).astype(BF).astype(F32)
    low = bias1 - high - mid
    built = outside1[...].astype(F32)
    for i, part in enumerate((high, mid, low)):
        built = built + part * bias_at[i].astype(F32)
    for i in range(9):
        picked = lax.dot_general(
            pick1[...], k1[i // 3][:, i % 3, :], (((1,), (1,)), ((), ())),
            preferred_element_type=F32)
        placed = dot(picked.astype(BF), place1[...])
        built = built + placed * mask1[i].astype(F32)
    w1[...] = built.astype(BF)
    blocks_row = [[jnp.zeros((oz, 3 * oz), BF)] * 4 for _ in range(2)]
    for b in range(3):
        band = jnp.zeros((oz, 3 * oz), F32)
        for a in range(3):
            taps = jnp.concatenate([k2[:, a, b, e, :] for e in range(3)], axis=1)
            placed = dot(dot(pick2[...], taps).astype(BF), place2[...])
            band = band + placed * mask2[a].astype(F32)
        band = band.astype(BF)
        for p in range(2):
            blocks_row[p][b + p] = band
    w2[...] = jnp.concatenate(
        [jnp.concatenate(blocks_row[p], axis=1) for p in range(2)], axis=0)
    wh[...] = (dot(dot(pick_h[...], kh[...]).astype(BF), place_h[...])
               * mask_h[...].astype(F32)).astype(BF)
    bias2[...] = jnp.concatenate(
        [jnp.full((zs, WIDE), b2[o], F32) for _ in range(2) for o in range(ch)], axis=0)
    bias_h[...] = jnp.concatenate(
        [jnp.full((zs * 8, LANES), bh[k], F32) for k in range(aff)], axis=0)


def exchange_kernel(
    secs, tiles, blocks, rows, count, *refs,
):
    far = refs[:count]
    out = refs[count]
    arrivals = refs[count + 1:count + 12]
    main, edge, top, bottom, stats, w1, w2, wh, bias2, bias_h, perm = arrivals
    near = refs[count + 12:2 * count + 11] + (perm,)
    shifted, first, load, stage, partial, strip, ends = refs[2 * count + 11:2 * count + 18]
    (send_m, recv_m, send_e, recv_e, send_t, recv_t, send_b, recv_b, send_s, recv_s) = refs[2 * count + 18:]
    loads = [pltpu.make_async_copy(far[i], near[i], load.at[i]) for i in range(count)]
    x_ref = near[0]
    s, t = lax.axis_index("sec"), lax.axis_index("tile")
    held = x_ref.shape[0]
    cols = x_ref.shape[2]
    staged = stage.shape[1]
    peers = secs * tiles
    home, place = t // blocks, t % blocks
    barrier = pltpu.get_barrier_semaphore()

    def greet(i, carry):
        s2, t2 = i // tiles, i % tiles

        @pl.when(jnp.logical_or(s2 != s, t2 != t))
        def _():
            pl.semaphore_signal(barrier, inc=1, device_id={"sec": s2, "tile": t2},
                                device_id_type=pl.DeviceIdType.MESH)

        return carry

    for copy in loads:
        copy.start()
    lax.fori_loop(0, peers, greet, 0)

    @pl.when(s == 0)
    def _():
        top[...] = jnp.zeros_like(top)

    @pl.when(s == secs - 1)
    def _():
        bottom[...] = jnp.zeros_like(bottom)

    loads[0].wait()
    sums = []
    squares = []
    groups = staged // 16
    strips = [jnp.zeros((16, LANES), F32)] * tiles
    halo_lane = lax.broadcasted_iota(jnp.int32, (16, LANES), 1) < 4
    firsts, lasts = [], []
    for i in range(held):
        values = x_ref[i].astype(F32)
        moved = pltpu.roll(values, 2, 1)
        moved = jnp.concatenate([moved, moved[:, :LANES]], axis=1)
        firsts.append(moved[:8])
        lasts.append(moved[rows - 8:])
        if staged > rows:
            moved = jnp.concatenate(
                [moved, jnp.zeros((staged - rows, cols + LANES), F32)], axis=0)
        stage[i] = moved.astype(BF)
        for c in range(tiles):
            for q in range(groups):
                kept = jnp.where(
                    halo_lane, moved[16 * q:16 * q + 16, (c + 1) * LANES:(c + 2) * LANES], 0.0)
                turn = 4 * (i * groups + q)
                strips[c] = strips[c] + (pltpu.roll(kept, turn, 1) if turn else kept)
        col_sum = jnp.sum(values, axis=0, keepdims=True)
        col_square = jnp.sum(values * values, axis=0, keepdims=True)
        sums.append(sum(col_sum[:, c:c + LANES] for c in range(0, cols, LANES)))
        squares.append(sum(col_square[:, c:c + LANES] for c in range(0, cols, LANES)))
    ends[0] = jnp.concatenate(firsts, axis=0).astype(BF)
    ends[1] = jnp.concatenate(lasts, axis=0).astype(BF)
    for c in range(tiles):
        strip[c] = strips[c].astype(BF)
    packed = jnp.concatenate(
        sums + squares + [jnp.zeros((8 - 2 * held, LANES), F32)], axis=0)
    partial[...] = packed

    def remote(src, dst, send, recv, s2, t2):
        return pltpu.make_async_remote_copy(
            src_ref=src, dst_ref=dst, send_sem=send, recv_sem=recv,
            device_id={"sec": s2, "tile": t2}, device_id_type=pl.DeviceIdType.MESH)

    def begin(wanted, src, dst, send, recv, s2, t2):
        own = jnp.logical_and(s2 == s, t2 == t)

        @pl.when(jnp.logical_and(wanted, jnp.logical_not(own)))
        def _():
            remote(src, dst, send, recv, s2, t2).start()

        @pl.when(jnp.logical_and(wanted, own))
        def _():
            pltpu.make_async_copy(src, dst, recv).start()

    def sent(wanted, src, dst, send, recv, s2, t2):
        own = jnp.logical_and(s2 == s, t2 == t)

        @pl.when(jnp.logical_and(wanted, jnp.logical_not(own)))
        def _():
            remote(src, dst, send, recv, s2, t2).wait_send()

    def arrived(wanted, src, dst, send, recv, s2, t2):
        own = jnp.logical_and(s2 == s, t2 == t)

        @pl.when(jnp.logical_and(wanted, jnp.logical_not(own)))
        def _():
            remote(src, dst, send, recv, s2, t2).wait_recv()

        @pl.when(jnp.logical_and(wanted, own))
        def _():
            pltpu.make_async_copy(src, dst, recv).wait()

    pl.semaphore_wait(barrier, peers - 1)
    mine = pl.ds(s * held, held)
    goes_up = jnp.logical_and(place == 0, home > 0)
    goes_down = jnp.logical_and(place == blocks - 1, home < secs - 1)

    def out_stats(act):
        def body(i, carry):
            s2, t2 = i // tiles, i % tiles
            act(s2 >= 0, partial, stats.at[t, s], send_s.at[i], recv_s.at[s, t], s2, t2)
            return carry

        lax.fori_loop(0, peers, body, 0)

    def out_pixels(act):
        def body(t2, carry):
            window = pl.ds(pl.multiple_of(t2 * LANES, LANES), WIDE)
            block = pl.ds(pl.multiple_of(t2 * LANES, LANES), LANES)
            act(t2 >= 0, stage.at[:, :, block], main.at[place, mine],
                send_m.at[t2], recv_m.at[s, place], home, t2)
            act(t2 >= 0, strip.at[t2], edge.at[place, s],
                send_e.at[t2], recv_e.at[s, place], home, t2)
            act(goes_up, ends.at[0, :, window], bottom.at[s],
                send_b.at[t2], recv_b.at[s], home - 1, t2)
            act(goes_down, ends.at[1, :, window],
                top.at[s], send_t.at[t2], recv_t.at[s], home + 1, t2)
            return carry

        lax.fori_loop(0, tiles, body, 0)

    out_pixels(begin)
    out_stats(begin)
    for copy in loads[1:]:
        copy.wait()
    build_weights(main.shape[1], *near[1:-1], w1, w2, wh, bias2, bias_h)

    def in_pixels(s2, carry):
        window = pl.ds(pl.multiple_of(t * LANES, LANES), WIDE)
        columns = pl.ds(pl.multiple_of(t * LANES, LANES), LANES)
        theirs = pl.ds(s2 * held, held)

        def block(k, inner):
            arrived(s2 >= 0, stage.at[:, :, columns], main.at[k, theirs],
                    send_m.at[0], recv_m.at[s2, k], s2, s * blocks + k)
            arrived(s2 >= 0, strip.at[t], edge.at[k, s2],
                    send_e.at[0], recv_e.at[s2, k], s2, s * blocks + k)
            return inner

        lax.fori_loop(0, blocks, block, 0)
        arrived(s > 0, ends.at[1, :, window],
                top.at[s2], send_t.at[0], recv_t.at[s2], s2, s * blocks - 1)
        arrived(s < secs - 1, ends.at[0, :, window], bottom.at[s2],
                send_b.at[0], recv_b.at[s2], s2, (s + 1) * blocks)
        return carry

    lax.fori_loop(0, secs, in_pixels, 0)

    def in_stats(i, carry):
        s2, t2 = i // tiles, i % tiles
        arrived(s2 >= 0, partial, stats.at[t2, s2], send_s.at[0], recv_s.at[s2, t2], s2, t2)
        return carry

    lax.fori_loop(0, peers, in_stats, 0)
    cells = rows * tiles * cols
    compute_kernel(secs, tiles, rows, cells, *arrivals, out, shifted, first)
    out_pixels(sent)
    out_stats(sent)


SLOTS = 6
OUTSIDE = -1e30


def tables(zs, ch, aff):
    oz = ch * zs
    o_of = np.arange(oz) // zs
    z_of = np.arange(oz) % zs
    perm = np.zeros((zs * 16, zs * 16), np.float32)
    for y in range(16):
        for z in range(zs):
            perm[y * zs + z, z * 16 + y] = 1
    rows_pick = (o_of[:, None] == np.arange(ch)[None]).astype(np.float32)
    pick1 = np.tile(rows_pick, (3, 1))
    e1 = np.arange(3 * oz) // oz
    z1 = np.tile(z_of, 3)
    col = np.arange(3 * SLOTS * zs)
    b_col, slot, z_col = col // (SLOTS * zs), col // zs % SLOTS, col % zs
    place1 = (np.arange(3)[:, None] == b_col[None]).astype(np.float32)
    mask1 = np.zeros((9, 3 * oz, col.size), np.float32)
    for a in range(3):
        for e in range(3):
            mask1[a * 3 + e] = (
                (z_col[None] - z1[:, None] + 1 == a)
                & (slot[None] - e1[:, None] == e) & (slot[None] < 5))
    aux = (b_col == 1) & (slot == 5)
    bias_at = np.stack([(aux & (z_col == i)) for i in range(3)]).astype(np.float32)
    outside1 = np.where(
        aux[None] & (z_col[None] == 3 + e1[:, None]), OUTSIDE, 0.0).astype(np.float32)
    col2 = np.arange(3 * oz)
    ec = col2 // zs
    place2 = (np.arange(3 * ch)[:, None] == ec[None]).astype(np.float32)
    mask2 = np.stack(
        [(col2 % zs)[None] - z_of[:, None] + 1 == a for a in range(3)]).astype(np.float32)
    row = np.arange(aff * zs * 8)
    pick_h = ((row // (zs * 8))[:, None] == np.arange(aff)[None]).astype(np.float32)
    col_h = np.arange(8 * oz)
    place_h = (np.arange(ch)[:, None] == (col_h // zs % ch)[None]).astype(np.float32)
    mask_h = (
        ((row // 8 % zs)[:, None] == (col_h % zs)[None])
        & ((row % 8)[:, None] == (col_h // oz)[None])).astype(np.float32)
    as_bf = lambda v: jnp.asarray(v.astype(jnp.bfloat16))
    return [as_bf(v) for v in (
        perm, rows_pick, pick1, place1, mask1, bias_at[:, None, :], outside1, place2, mask2,
        pick_h, place_h, mask_h)]


def exchange(x, k1, b1, k2, b2, kh, bh, secs, tiles):
    held, rows, cols = x.shape
    brick_rows = rows * tiles // secs
    blocks = brick_rows // rows
    staged = max(rows, HALO_ROWS)
    zs = held * secs
    ch, aff = b1.shape[0], bh.shape[0]
    oz = ch * zs
    k1 = jnp.transpose(k1[:, 0], (1, 2, 3, 0))
    k2 = jnp.transpose(k2, (0, 2, 3, 4, 1))
    perm, *consts = tables(zs, ch, aff)
    operands = [x, k1, k2, kh, b1, b2, bh, *consts, perm]
    dma = pltpu.SemaphoreType.DMA
    vmem = pl.BlockSpec(memory_space=pltpu.VMEM)
    hbm = pl.BlockSpec(memory_space=pltpu.HBM)
    near = [
        (pltpu.SMEM if v.ndim == 1 else pltpu.VMEM)(v.shape, v.dtype) for v in operands[:-1]]
    return pl.pallas_call(
        functools.partial(exchange_kernel, secs, tiles, blocks, rows, len(operands)),
        out_shape=jax.ShapeDtypeStruct((aff, zs, brick_rows, LANES), F32),
        in_specs=[hbm] * len(operands),
        out_specs=vmem,
        scratch_shapes=[
            pltpu.VMEM((blocks, zs, staged, LANES), BF),
            pltpu.VMEM((blocks, secs, 16, LANES), BF),
            pltpu.VMEM((secs, 8 * held, WIDE), BF),
            pltpu.VMEM((secs, 8 * held, WIDE), BF),
            pltpu.VMEM((tiles, secs, 8, LANES), F32),
            pltpu.VMEM((3 * oz, 3 * SLOTS * zs), BF),
            pltpu.VMEM((2 * oz, 12 * oz), BF),
            pltpu.VMEM((aff * zs * 8, 8 * oz), BF),
            pltpu.VMEM((2 * oz, WIDE), F32),
            pltpu.VMEM((aff * zs * 8, LANES), F32),
            pltpu.VMEM(perm.shape, BF),
        ] + near + [
            pltpu.VMEM((brick_rows + 4, SLOTS * zs, LANES), BF),
            pltpu.VMEM((brick_rows + 2, 3 * oz, LANES), BF),
            dma((len(operands),)),
            pltpu.VMEM((held, staged, cols + LANES), BF),
            pltpu.VMEM((8, LANES), F32),
            pltpu.VMEM((tiles, 16, LANES), BF),
            pltpu.VMEM((2, 8 * held, cols + LANES), BF),
            dma((tiles,)), dma((secs, blocks)),
            dma((tiles,)), dma((secs, blocks)),
            dma((tiles,)), dma((secs,)),
            dma((tiles,)), dma((secs,)),
            dma((secs * tiles,)), dma((secs, tiles)),
        ],
        compiler_params=pltpu.CompilerParams(
            collective_id=0, has_side_effects=True, vmem_limit_bytes=60 * 2**20),
        name="predict",
    )(*operands)


def compute_kernel(
    secs, tiles, rows, cells, main, edge, top, bottom, stats, w1, w2, wh, bias2, bias_h, perm,
    out, shifted, first,
):
    s, t = lax.axis_index("sec"), lax.axis_index("tile")
    aff, zs, brick_rows, brick_cols = out.shape
    blocks, _, staged, _ = main.shape
    held = zs // secs
    oz = w1.shape[0] // 3

    summed = jnp.sum(stats[...], axis=0)
    summed = jnp.sum(summed, axis=2, keepdims=True)
    total = jnp.concatenate([summed[i, 0:held] for i in range(secs)], axis=0)
    square = jnp.concatenate([summed[i, held:2 * held] for i in range(secs)], axis=0)
    average = total / cells
    variance = square / cells - average * average
    inv_std = jnp.broadcast_to(lax.rsqrt(variance + 1e-05), (zs, WIDE))
    average = jnp.broadcast_to(average, (zs, WIDE))

    lane = lax.broadcasted_iota(jnp.int32, (16, zs, WIDE), 2) - 2 + t * brick_cols
    col_inside = (lane >= 0) & (lane < brick_cols * tiles)
    slot = lax.broadcasted_iota(jnp.int32, (16, zs, LANES), 1)
    x_at = lax.broadcasted_iota(jnp.int32, (16, zs, LANES), 2) + t * brick_cols
    y_in = lax.broadcasted_iota(jnp.int32, (16, zs, LANES), 0)
    x_seen = x_at + slot - 4
    x_outside = (x_seen < 0) | (x_seen >= brick_cols * tiles)

    def spread(raw, row0, inside):
        turned = dot(perm[...], raw.reshape(zs * 16, WIDE)).reshape(16, zs, WIDE)
        normed = (turned - average[None]) * inv_std[None]
        normed = jnp.where(col_inside & inside, normed, 0.0).reshape(16 * zs, WIDE)
        parts = [normed[:, :LANES]]
        for i in range(1, 5):
            parts.append(pltpu.roll(normed, WIDE - i, 1)[:, :LANES])
        y_at = y_in + row0 + s * brick_rows
        y_outside = (y_at < 0) | (y_at >= brick_rows * secs)
        aux = jnp.where(
            slot < 3, 1.0, jnp.where((slot < 6) & (y_outside | x_outside), 1.0, 0.0))
        parts = [part.reshape(16, zs, LANES) for part in parts] + [aux]
        return jnp.concatenate(parts, axis=1).astype(BF)

    step = min(rows, 16)
    for k in range(blocks):
        for q in range(staged // 16):
            row0 = k * rows + q * 16
            halo = []
            for z in range(zs):
                turn = 4 * (z % held * (staged // 16) + q)
                strip = edge[k, z // held].astype(F32)
                halo.append(pltpu.roll(strip, LANES - turn, 1) if turn else strip)
            halo = jnp.concatenate(halo, axis=0).astype(BF).reshape(zs, 16, LANES)
            ready = spread(jnp.concatenate(
                [main[k, :, q * 16:q * 16 + 16, :], halo], axis=2), row0, True)
            shifted[2 + row0:2 + row0 + step] = ready[:step]

    def filled(halo_rows):
        held_rows = halo_rows[...].astype(F32).reshape(zs, 8, WIDE)
        return jnp.concatenate([held_rows, jnp.zeros_like(held_rows)], axis=1).astype(BF)

    shifted[0:2] = spread(filled(top), -8, s > 0)[6:8]
    shifted[2 + brick_rows:4 + brick_rows] = spread(
        filled(bottom), brick_rows, s < secs - 1)[0:2]

    depth1 = w1.shape[1]

    def layer_one(i, carry):
        j = 2 * i
        x = jnp.concatenate(
            [shifted[pl.ds(j + d, 3)].reshape(depth1, LANES) for d in range(2)], axis=1)
        y = jnp.maximum(dot(w1[...], x), 0.0).astype(BF)
        first[j] = y[:, :LANES]
        first[j + 1] = y[:, LANES:]
        return carry

    lax.fori_loop(0, (brick_rows + 2) // 2, layer_one, 0, unroll=3)

    def layer_two(i, carry):
        found = []
        for h in range(2):
            j = 8 * i + 4 * h
            x = jnp.concatenate(
                [first[pl.ds(j + d, 4)].reshape(12 * oz, LANES) for d in (0, 2)], axis=1)
            y = jnp.maximum(dot(w2[...], x) + bias2[...], 0.0).astype(BF)
            found += [y[:, :LANES], y[:, LANES:]]
        logits = dot(wh[...], jnp.concatenate(found, axis=0)) + bias_h[...]
        out[:, :, pl.ds(pl.multiple_of(8 * i, 8), 8), :] = jax.nn.sigmoid(logits).reshape(
            aff, zs, 8, LANES)
        return carry

    lax.fori_loop(0, brick_rows // 8, layer_two, 0, unroll=2)


def per_device(
    sections_in, first_kernel, first_bias, second_kernel, second_bias, head_kernel, head_bias
):
    secs, tiles = lax.axis_size("sec"), lax.axis_size("tile")
    return exchange(
        sections_in, first_kernel, first_bias, second_kernel, second_bias, head_kernel,
        head_bias, secs, tiles)


def solution(mesh):
    in_specs = (P("sec", "tile", "half"), P(), P(), P(), P(), P(), P())
    out_specs = P(None, None, "sec", ("half", "tile"))
    return jax.shard_map(
        per_device, mesh=mesh, in_specs=in_specs, out_specs=out_specs, check_vma=False
    )
```
